32 devices in a mesh: pair: 2 (over x), dp: 2 (over y), vocab: 8 (over z, core).
Axes of the slice: x: 2, y: 2, z: 4, core: 2. Of those that a mesh axis runs over, the one named last changes fastest.
Arguments:
- hidden: bfloat16 [2, 48, 8192], P(None, None, ('pair', 'dp')), may hold values from -64 to 64
- head_weight: bfloat16 [8192, 16384], P(('pair', 'dp'), 'vocab'), may hold values from -2 to 2
- answer_mask: int32 [48], replicated, may hold values 0 or 1
Outputs:
- grad_hidden: float32 [96, 8192], P('vocab', ('pair', 'dp'))
- kl_rows: float32 [48], P('dp')
The draws below stay inside these ranges and needn't reach their ends.
All inputs are finite; a program needn't handle non-finite values.
Results may differ from the reference program's by a relative error of at most 0.0003.
Values sent between devices are 32-bit elements; how exact they have to be, the bound alone decides.
A program may use at most 64 MiB of HBM per device.

```python
import math
import jax
import jax.numpy as jnp
from jax import lax

D = 8192
V_DEV = 2048
TOKENS = 48
VOCAB = 16384


def signs_table(key):
    return jax.random.rademacher(jax.random.fold_in(key, 3), (VOCAB // V_DEV, D), dtype=jnp.float32)


def alternate():
    return 1.0 - 2.0 * (jnp.arange(D) % 2).astype(jnp.float32)


def drawn_scale():
    return min(1.0, 11.0 / math.sqrt(D))


def draw_head_weight(key, part):
    slabs = VOCAB // V_DEV
    values = jnp.clip(jax.random.normal(jax.random.fold_in(key, 1), (D, VOCAB), jnp.float32), -6.0, 6.0)
    frac = jnp.arange(VOCAB).astype(jnp.float32) / VOCAB
    scales = jnp.exp(jax.random.uniform(jax.random.fold_in(key, 2), (VOCAB,), jnp.float32, math.log(0.2), math.log(1.0))) * (0.5 + frac)
    signs = signs_table(key)
    values = values.reshape(D, slabs, V_DEV)
    values = values.at[:, :, 0].set(signs.T).at[:, :, 1].set((signs * alternate()[None, :]).T)
    values = values.reshape(D, VOCAB)
    scales = scales.reshape(slabs, V_DEV).at[:, 0:2].set(drawn_scale()).reshape(VOCAB)
    return (values * scales[None, :] / math.sqrt(D)).astype(jnp.bfloat16)


def draw_hidden(key, part):
    slabs = VOCAB // V_DEV
    rowscale = jnp.exp(jax.random.uniform(jax.random.fold_in(key, 4), (TOKENS, 1), jnp.float32, math.log(0.3), math.log(3.0)))
    base = jnp.clip(jax.random.normal(jax.random.fold_in(key, 5), (TOKENS, D), jnp.float32), -6.0, 6.0)
    noise = jnp.clip(jax.random.normal(jax.random.fold_in(key, 7), (TOKENS, D), jnp.float32), -6.0, 6.0)
    levels_table = jnp.array([16.0, 20.0, 26.0], jnp.float32)
    clean = base * rowscale
    adverse = clean + rowscale * noise
    positions = jnp.arange(TOKENS)
    picked = (positions % 16 == 3)[:, None]
    levels = levels_table[positions // 16 % 3][:, None]
    chosen = jax.random.randint(jax.random.fold_in(key, 8), (TOKENS,), 0, slabs)
    rows_sign = signs_table(key)[chosen]
    aligned = (levels * rows_sign + (levels - 2.0) * rows_sign * alternate()[None, :]) / (drawn_scale() * math.sqrt(D))
    clean = jnp.where(picked, aligned, clean)
    adverse = jnp.where(picked, aligned + 0.5 * noise, adverse)
    return jnp.clip(jnp.stack([clean, adverse]), -64.0, 64.0).astype(jnp.bfloat16)


def touch_ends(drawn, stream_key, least, high):
    spot = [jax.random.randint(jax.random.fold_in(stream_key, axis), (), 0, length) for axis, length in enumerate(drawn.shape)]
    widest = drawn.shape.index(max(drawn.shape))
    neighbour = spot[:widest] + [(spot[widest] + 1) % drawn.shape[widest]] + spot[widest + 1:]
    return drawn.at[tuple(spot)].set(least).at[tuple(neighbour)].set(high)


def setup_inputs(seed: int = 0) -> dict:
    seeds = jax.random.split(jax.random.key(seed), 4)
    hidden = draw_hidden(jax.random.fold_in(seeds[3], 71), 0)
    head_weight = draw_head_weight(jax.random.fold_in(seeds[3], 71), 0)
    answer_mask = touch_ends((jax.random.randint(seeds[2], (TOKENS,), 0, 4) < 3).astype(jnp.int32), jax.random.fold_in(seeds[2], 1), 0, 1)
    return dict(hidden=hidden, head_weight=head_weight, answer_mask=answer_mask)


trades_scale = 6.0


def reference(hidden, head_weight, answer_mask):
    slabs = VOCAB // V_DEV
    flat = hidden.reshape(2 * TOKENS, D).astype(jnp.float32)

    def slab_logits(index):
        block = lax.dynamic_slice_in_dim(head_weight, index * V_DEV, V_DEV, 1).astype(jnp.float32)
        return jnp.dot(flat, block, precision=lax.Precision.HIGHEST)

    logits = lax.map(slab_logits, jnp.arange(slabs, dtype=jnp.int32))
    logits = jnp.transpose(logits, (1, 0, 2)).reshape(2 * TOKENS, VOCAB)
    row_top = jnp.max(logits, axis=1, keepdims=True)
    lse = row_top + jnp.log(jnp.sum(jnp.exp(logits - row_top), axis=1, keepdims=True))
    logp = logits - lse
    clean_logp = logp[:TOKENS]
    adv_logp = logp[TOKENS:]
    clean_prob = jnp.exp(clean_logp)
    kl_full = jnp.sum(clean_prob * (clean_logp - adv_logp), axis=1)
    mask_float = answer_mask.astype(jnp.float32)
    kl_rows = mask_float * kl_full
    weight = (trades_scale * mask_float)[:, None]
    clean_grad = weight * clean_prob * (clean_logp - adv_logp - kl_full[:, None])
    adv_grad = weight * (jnp.exp(adv_logp) - clean_prob)
    logit_grad = jnp.concatenate([clean_grad, adv_grad], axis=0)

    def add_slab(carry, index):
        block = lax.dynamic_slice_in_dim(head_weight, index * V_DEV, V_DEV, 1).astype(jnp.float32)
        grads = lax.dynamic_slice_in_dim(logit_grad, index * V_DEV, V_DEV, 1)
        return carry + jnp.dot(grads, block.T, precision=lax.Precision.HIGHEST), None

    grad_hidden, unused = lax.scan(add_slab, jnp.zeros((2 * TOKENS, D), jnp.float32), jnp.arange(slabs, dtype=jnp.int32))
    return grad_hidden, kl_rows
```

```python
import functools

import jax
import jax.numpy as jnp
from jax import lax
from jax.experimental import pallas as pl
from jax.experimental.pallas import tpu as pltpu
from jax.sharding import PartitionSpec as P

trades_scale = 6.0
MESH = pl.DeviceIdType.MESH
F32 = jnp.float32
BF16 = jnp.bfloat16


def merge(parts):
    top_c = functools.reduce(jnp.maximum, [p[0] for p in parts])
    top_a = functools.reduce(jnp.maximum, [p[3] for p in parts])
    total_c = total_a = cross = 0.0
    for m_c, s_c, t, m_a, s_a in parts:
        down_c, down_a = m_c - top_c, m_a - top_a
        e_c = jnp.exp(down_c)
        total_c += e_c * s_c
        total_a += jnp.exp(down_a) * s_a
        cross += e_c * (t + s_c * (down_c - down_a))
    return top_c, total_c, cross, top_a, total_a


def pack(stats):
    rows = stats[0].shape[0]
    lane = lax.broadcasted_iota(jnp.int32, (rows, 128), 1)
    out = jnp.zeros((rows, 128), F32)
    for j, s in enumerate(stats):
        out = jnp.where(lane == j, s, out)
    return out


def unpack(value):
    return tuple(value[:, j : j + 1] for j in range(5))


def kernel(
    n_pair, n_dp, n_v,
    h_ref, w_ref, mask_ref,
    grad_ref, kl_ref,
    wbuf, part, rs_in, gath, gbuf, st_a, st_b, acc, core_in, z_in, z_own, c2_in,
    w_sem, rs_s, rs_r, ag_s, ag_r, sa_s, sa_r, sb_s, sb_r, c1_s, c1_r, z_s, z_r, c2_s, c2_r,
):
    n_xy = n_pair * n_dp
    n_hi = n_v // 2
    rows, depth = h_ref.shape
    tokens = rows // 2
    cols = wbuf.shape[2]
    half = depth // 2
    block = rows // n_hi
    px, py, v = lax.axis_index("pair"), lax.axis_index("dp"), lax.axis_index("vocab")
    hi, lo = v // 2, v % 2

    shifts = [(i // n_dp, i % n_dp) for i in range(n_xy)]
    peers = [
        (lax.rem(px + sx, n_pair), lax.rem(py + sy, n_dp)) for sx, sy in shifts
    ]
    minus = [((-sx) % n_pair) * n_dp + (-sy) % n_dp for sx, sy in shifts]
    order = sorted(range(1, n_xy), key=lambda i: -(shifts[i][0] + shifts[i][1]))

    def xy_id(i):
        return (peers[i][0], peers[i][1], v)

    def v_id(j):
        return (px, py, lax.rem(v + j, n_v))

    partner = (px, py, hi * 2 + (1 - lo))

    def hi_id(j):
        return (px, py, lax.rem(hi + j, n_hi) * 2 + lo)

    loads = {}
    for i in order + [0]:
        q = peers[i][0] * n_dp + peers[i][1]
        loads[i] = pltpu.make_async_copy(
            w_ref.at[:, pl.ds(pl.multiple_of(q * cols, 128), cols)], wbuf.at[i], w_sem.at[i]
        )
        loads[i].start()

    barrier = pltpu.get_barrier_semaphore()
    for i in range(1, n_xy):
        pl.semaphore_signal(barrier, inc=1, device_id=xy_id(i), device_id_type=MESH)
    for j in range(1, n_v):
        pl.semaphore_signal(barrier, inc=1, device_id=v_id(j), device_id_type=MESH)

    def remote(src, dst, send, recv, to):
        return pltpu.make_async_remote_copy(
            src_ref=src, dst_ref=dst, send_sem=send, recv_sem=recv, device_id=to, device_id_type=MESH
        )

    rs = {}
    for n, i in enumerate(order + [0]):
        loads[i].wait()
        part[i] = jnp.dot(h_ref[...], wbuf[i], preferred_element_type=F32)
        if n == 0:
            pl.semaphore_wait(barrier, n_xy - 1 + n_v - 1)
        if i:
            rs[i] = remote(part.at[i], rs_in.at[i], rs_s.at[i], rs_r.at[i], xy_id(i))
            rs[i].start()
    own = part[0]
    for i in order[::-1]:
        rs[i].wait_recv()
        own = own + rs_in[i]
    gath[0] = own
    ag = {}
    for i in order:
        ag[i] = remote(gath.at[0], gath.at[i], ag_s.at[i], ag_r.at[i], xy_id(i))
        ag[i].start()

    l_c, l_a = own[:tokens], own[tokens:]
    m_c = jnp.max(l_c, axis=1, keepdims=True)
    m_a = jnp.max(l_a, axis=1, keepdims=True)
    l_c, l_a = l_c - m_c, l_a - m_a
    e_c = jnp.exp(l_c)
    st_a[0] = pack((
        m_c,
        jnp.sum(e_c, axis=1, keepdims=True),
        jnp.sum(e_c * (l_c - l_a), axis=1, keepdims=True),
        m_a,
        jnp.sum(jnp.exp(l_a), axis=1, keepdims=True),
    ))
    sa = {}
    for j in range(1, n_v):
        sa[j] = remote(st_a.at[0], st_a.at[j], sa_s.at[j], sa_r.at[j], v_id(j))
        sa[j].start()
    for j in range(1, n_v):
        sa[j].wait_recv()
    st_b[0] = pack(merge([unpack(st_a[j]) for j in range(n_v)]))
    sb = {}
    for i in order:
        sb[i] = remote(st_b.at[0], st_b.at[i], sb_s.at[i], sb_r.at[i], xy_id(i))
        sb[i].start()

    row_iota = lax.broadcasted_iota(jnp.int32, (tokens, tokens), 0)
    col_iota = lax.broadcasted_iota(jnp.int32, (tokens, tokens), 1)
    mask = jnp.sum(
        jnp.where(row_iota == col_iota, mask_ref[...].astype(F32), 0.0), axis=1, keepdims=True
    )
    weight = trades_scale * mask

    for i in order:
        sb[i].wait_recv()
    top_c, total_c, cross, top_a, total_a = merge([unpack(st_b[i]) for i in range(n_xy)])
    log_c, log_a = jnp.log(total_c), jnp.log(total_a)
    kl = cross / total_c - log_c + log_a
    group = kl_ref.shape[1]
    token = lax.broadcasted_iota(jnp.int32, (tokens, group), 0)
    place = lax.broadcasted_iota(jnp.int32, (tokens, group), 1) + py * group
    kl_ref[...] = jnp.sum(jnp.where(token == place, mask * kl, 0.0), axis=0, keepdims=True)

    step = min(512, half)
    near = pl.multiple_of(lo * half, 128)
    far = pl.multiple_of((1 - lo) * half, 128)
    for n, i in enumerate([0] + order[::-1]):
        if i:
            ag[i].wait_recv()
        x_c = (gath[i, :tokens] - top_c) - log_c
        x_a = (gath[i, tokens:] - top_a) - log_a
        p_c = jnp.exp(x_c)
        g_c = weight * p_c * (x_c - x_a - kl)
        g_a = weight * (jnp.exp(x_a) - p_c)
        for k, g in enumerate((g_c, g_a)):
            high = g.astype(BF16)
            gbuf[pl.ds(k * tokens, tokens), :] = high
            gbuf[pl.ds(rows + k * tokens, tokens), :] = (g - high.astype(F32)).astype(BF16)
        for side, start in ((1, far), (0, near)):
            for d in range(0, half, step):
                both = lax.dot_general(
                    gbuf[...],
                    wbuf[minus[i], pl.ds(pl.multiple_of(start + d, 128), step), :],
                    (((1,), (1,)), ((), ())),
                    preferred_element_type=F32,
                )
                both = both[:rows] + both[rows:]
                if n == 0:
                    acc[side, :, d : d + step] = both
                else:
                    acc[side, :, d : d + step] += both
            if side and n == n_xy - 1:
                c1 = remote(acc.at[1], core_in, c1_s, c1_r, partner)
                c1.start()

    c1.wait_recv()
    acc[0] += core_in[...]
    zs = {}
    for j in range(n_hi - 1, 0, -1):
        to = lax.rem(hi + j, n_hi)
        zs[j] = remote(
            acc.at[0, pl.ds(pl.multiple_of(to * block, 8), block)],
            z_in.at[j], z_s.at[j], z_r.at[j], hi_id(j),
        )
        zs[j].start()
    total = acc[0, pl.ds(pl.multiple_of(hi * block, 8), block), :]
    for j in range(1, n_hi):
        zs[j].wait_recv()
        total = total + z_in[j]
    z_own[...] = total
    c2 = remote(z_own, c2_in, c2_s, c2_r, partner)
    c2.start()
    c2.wait_recv()
    out = block // 2
    first = lo == 0
    mine = jnp.where(first, z_own[:out], z_own[out:])
    theirs = jnp.where(first, c2_in[:out], c2_in[out:])
    grad_ref[:, :half] = jnp.where(first, mine, theirs)
    grad_ref[:, half:] = jnp.where(first, theirs, mine)

    for i in order:
        rs[i].wait_send()
        ag[i].wait_send()
        sb[i].wait_send()
    for j in range(1, n_v):
        sa[j].wait_send()
    for j in range(1, n_hi):
        zs[j].wait_send()
    c1.wait_send()
    c2.wait_send()


def solution(mesh):
    n_pair, n_dp, n_v = (mesh.shape[a] for a in ("pair", "dp", "vocab"))
    n_xy, n_hi = n_pair * n_dp, n_v // 2

    def per_device(hidden, head_weight, answer_mask):
        tokens = hidden.shape[1]
        rows = 2 * tokens
        depth, slab = head_weight.shape
        cols = slab // n_xy
        half = depth // 2
        block = rows // n_hi
        dma = pltpu.SemaphoreType.DMA
        vmem = pl.BlockSpec(memory_space=pltpu.VMEM)
        grad, kl = pl.pallas_call(
            functools.partial(kernel, n_pair, n_dp, n_v),
            out_shape=(
                jax.ShapeDtypeStruct((rows // n_v, depth), F32),
                jax.ShapeDtypeStruct((1, tokens // n_dp), F32),
            ),
            in_specs=[vmem, pl.BlockSpec(memory_space=pl.ANY), vmem],
            out_specs=(vmem, vmem),
            scratch_shapes=[
                pltpu.VMEM((n_xy, depth, cols), BF16),
                pltpu.VMEM((n_xy, rows, cols), F32),
                pltpu.VMEM((n_xy, rows, cols), F32),
                pltpu.VMEM((n_xy, rows, cols), F32),
                pltpu.VMEM((2 * rows, cols), BF16),
                pltpu.VMEM((n_v, tokens, 128), F32),
                pltpu.VMEM((n_xy, tokens, 128), F32),
                pltpu.VMEM((2, rows, half), F32),
                pltpu.VMEM((rows, half), F32),
                pltpu.VMEM((n_hi, block, half), F32),
                pltpu.VMEM((block, half), F32),
                pltpu.VMEM((block, half), F32),
                dma((n_xy,)),
                dma((n_xy,)), dma((n_xy,)),
                dma((n_xy,)), dma((n_xy,)),
                dma((n_v,)), dma((n_v,)),
                dma((n_xy,)), dma((n_xy,)),
                dma, dma,
                dma((n_hi,)), dma((n_hi,)),
                dma, dma,
            ],
            compiler_params=pltpu.CompilerParams(
                collective_id=0, has_side_effects=True, vmem_limit_bytes=48 * 2**20
            ),
        )(hidden.reshape(rows, depth), head_weight, answer_mask.reshape(1, tokens))
        return grad, kl.reshape(-1)

    return jax.shard_map(
        per_device,
        mesh=mesh,
        in_specs=(P(None, None, ("pair", "dp")), P(("pair", "dp"), "vocab"), P()),
        out_specs=(P("vocab", ("pair", "dp")), P("dp")),
        check_vma=False,
    )
```

```python
import functools

import jax
import jax.numpy as jnp
from jax import lax
from jax.experimental import pallas as pl
from jax.experimental.pallas import tpu as pltpu
from jax.sharding import PartitionSpec as P

trades_scale = 6.0
MESH = pl.DeviceIdType.MESH
F32 = jnp.float32
BF16 = jnp.bfloat16


def merge(parts):
    top_c = functools.reduce(jnp.maximum, [p[0] for p in parts])
    top_a = functools.reduce(jnp.maximum, [p[3] for p in parts])
    total_c = total_a = cross = 0.0
    for m_c, s_c, t, m_a, s_a in parts:
        down_c, down_a = m_c - top_c, m_a - top_a
        e_c = jnp.exp(down_c)
        total_c += e_c * s_c
        total_a += jnp.exp(down_a) * s_a
        cross += e_c * (t + s_c * (down_c - down_a))
    return top_c, total_c, cross, top_a, total_a


def pack(stats):
    place = lax.broadcasted_iota(jnp.int32, (8, stats[0].shape[1]), 0)
    out = jnp.zeros(place.shape, F32)
    for j, s in enumerate(stats):
        out = jnp.where(place == j, s, out)
    return out


def unpack(value):
    return tuple(value[j : j + 1, :] for j in range(5))


def kernel(
    n_pair, n_dp, n_v,
    h_any, w_ref, mask_any,
    grad_ref, kl_ref,
    h_ref, mask_ref, wbuf, part, rs_in, gath, gbuf, st_a, st_b, acc, core_in, z_in, z_own, c2_in,
    w_sem, in_sem, rs_s, rs_r, ag_s, ag_r, sa_s, sa_r, sb_s, sb_r, c1_s, c1_r, z_s, z_r, c2_s, c2_r,
):
    n_xy = n_pair * n_dp
    n_hi = n_v // 2
    rows, depth = h_ref.shape
    tokens = rows // 2
    few = tokens // 2
    wide = st_a.shape[2]
    cols = wbuf.shape[2]
    half = depth // 2
    block = rows // n_hi
    px, py, v = lax.axis_index("pair"), lax.axis_index("dp"), lax.axis_index("vocab")
    hi, lo = v // 2, v % 2

    shifts = [(i // n_dp, i % n_dp) for i in range(n_xy)]
    peers = [
        (lax.rem(px + sx, n_pair), lax.rem(py + sy, n_dp)) for sx, sy in shifts
    ]
    minus = [((-sx) % n_pair) * n_dp + (-sy) % n_dp for sx, sy in shifts]
    along_x = [sx * n_dp for sx in range(1, n_pair)]
    along_y = list(range(1, n_dp))
    across = [i for i in range(n_xy) if shifts[i][0] and shifts[i][1]]
    order = across + along_x + along_y + [0]

    def xy_id(i):
        return (peers[i][0], peers[i][1], v)

    def v_id(j):
        return (px, py, lax.rem(v + j, n_v))

    partner = (px, py, hi * 2 + (1 - lo))

    h_load = pltpu.make_async_copy(h_any, h_ref, in_sem.at[0])
    h_load.start()
    loads = {}
    for i in order:
        q = peers[i][0] * n_dp + peers[i][1]
        loads[i] = pltpu.make_async_copy(
            w_ref.at[:, pl.ds(pl.multiple_of(q * cols, 128), cols)], wbuf.at[i], w_sem.at[i]
        )
        loads[i].start()
    mask_load = pltpu.make_async_copy(mask_any, mask_ref, in_sem.at[1])
    mask_load.start()

    barrier = pltpu.get_barrier_semaphore()
    for i in range(1, n_xy):
        pl.semaphore_signal(barrier, inc=1, device_id=xy_id(i), device_id_type=MESH)
    for j in range(1, n_v):
        pl.semaphore_signal(barrier, inc=1, device_id=v_id(j), device_id_type=MESH)

    def remote(src, dst, send, recv, to):
        copy = pltpu.make_async_remote_copy(
            src_ref=src, dst_ref=dst, send_sem=send, recv_sem=recv, device_id=to, device_id_type=MESH
        )
        copy.start()
        return copy

    rs = {}

    def reduce_send(g, i, to):
        rs[g, i] = remote(part.at[g, i], rs_in.at[g, i], rs_s.at[g, i], rs_r.at[g, i], xy_id(to))

    h_load.wait()
    for n, i in enumerate(order):
        sx, sy = shifts[i]
        loads[i].wait()
        value = jnp.dot(h_ref[...], wbuf[i], preferred_element_type=F32)
        for g in range(2):
            for k in range(2):
                part[g, i, k] = value[k * tokens + g * few : k * tokens + (g + 1) * few]
        if n == 0:
            pl.semaphore_wait(barrier, n_xy - 1 + n_v - 1)
        if sx:
            reduce_send(0, i, sx * n_dp)
        if sy:
            reduce_send(1, i, sy)

    def take(g, i, source):
        rs[g, source].wait_recv()
        part[g, i] += rs_in[g, source]

    for sy in along_y:
        for sx in range(1, n_pair):
            take(0, sy, sx * n_dp + sy)
        reduce_send(0, sy, sy)
    for i in along_x:
        for sy in along_y:
            take(1, i, i + sy)
        reduce_send(1, i, i)

    ag = {}

    def gather_send(g):
        for i in along_x + along_y:
            ag[g, i, 0] = remote(
                gath.at[g, 0], gath.at[g, i], ag_s.at[g, i, 0], ag_r.at[g, i, 0], xy_id(i)
            )

    def gather_forward(g):
        for sy in along_y:
            ag[g, sy, 0].wait_recv()
            for i in along_x:
                ag[g, i + sy, 0] = remote(
                    gath.at[g, sy, 0], gath.at[g, i + sy, 0],
                    ag_s.at[g, i + sy, 0], ag_r.at[g, i + sy, 0], xy_id(i),
                )
        for i in along_x:
            ag[g, i, 0].wait_recv()
            for sy in along_y:
                ag[g, i + sy, 1] = remote(
                    gath.at[g, i, 1], gath.at[g, i + sy, 1],
                    ag_s.at[g, i + sy, 1], ag_r.at[g, i + sy, 1], xy_id(sy),
                )

    for i in along_x:
        take(0, 0, i)
    for i in along_y:
        take(1, 0, i)
    for i in along_y:
        rs[0, i].wait_recv()
    gath[0, 0] = part[0, 0] + sum(rs_in[0, i] for i in along_y)
    gather_send(0)
    for i in along_x:
        rs[1, i].wait_recv()
    gath[1, 0] = part[1, 0] + sum(rs_in[1, i] for i in along_x)

    diagonal = lax.broadcasted_iota(jnp.int32, (tokens, wide), 0) == lax.broadcasted_iota(
        jnp.int32, (tokens, wide), 1
    )

    def to_row(column):
        return jnp.sum(jnp.where(diagonal, column, 0.0), axis=0, keepdims=True)

    def to_column(row):
        return jnp.sum(jnp.where(diagonal, row, 0.0), axis=1, keepdims=True)

    l_c = jnp.concatenate([gath[0, 0, 0], gath[1, 0, 0]], axis=0)
    l_a = jnp.concatenate([gath[0, 0, 1], gath[1, 0, 1]], axis=0)
    m_c = jnp.max(l_c, axis=1, keepdims=True)
    m_a = jnp.max(l_a, axis=1, keepdims=True)
    l_c, l_a = l_c - m_c, l_a - m_a
    e_c = jnp.exp(l_c)
    stats = (
        m_c,
        jnp.sum(e_c, axis=1, keepdims=True),
        jnp.sum(e_c * (l_c - l_a), axis=1, keepdims=True),
        m_a,
        jnp.sum(jnp.exp(l_a), axis=1, keepdims=True),
    )
    st_a[0] = pack([to_row(s) for s in stats])
    sa = {}
    for j in range(1, n_v):
        sa[j] = remote(st_a.at[0], st_a.at[j], sa_s.at[j], sa_r.at[j], v_id(j))
    for j in range(1, n_v):
        sa[j].wait_recv()
    st_b[0] = pack(merge([unpack(st_a[j]) for j in range(n_v)]))
    sb = {}
    for i in range(1, n_xy):
        sb[i] = remote(st_b.at[0], st_b.at[i], sb_s.at[i], sb_r.at[i], xy_id(i))
    gather_forward(0)
    gather_send(1)

    mask_load.wait()
    mask = jnp.sum(
        jnp.where(diagonal[:, :tokens], mask_ref[...].astype(F32), 0.0), axis=1, keepdims=True
    )
    weight = trades_scale * mask
    for i in range(1, n_xy):
        sb[i].wait_recv()
    joined = merge([unpack(st_b[i]) for i in range(n_xy)])
    top_c, total_c, cross, top_a, total_a = (to_column(s) for s in joined)
    log_c, log_a = jnp.log(total_c), jnp.log(total_a)
    kl = cross / total_c - log_c + log_a
    group = kl_ref.shape[1]
    token = lax.broadcasted_iota(jnp.int32, (tokens, group), 0)
    place = lax.broadcasted_iota(jnp.int32, (tokens, group), 1) + py * group
    kl_ref[...] = jnp.sum(jnp.where(token == place, mask * kl, 0.0), axis=0, keepdims=True)

    step = min(512, half)
    near = pl.multiple_of(lo * half, 128)
    far = pl.multiple_of((1 - lo) * half, 128)

    def product(g):
        mine = slice(g * few, (g + 1) * few)
        for n, i in enumerate([0] + along_y + along_x + across):
            if i in across:
                ag[g, i, 0].wait_recv()
                ag[g, i, 1].wait_recv()
            x_c = (gath[g, i, 0] - top_c[mine]) - log_c[mine]
            x_a = (gath[g, i, 1] - top_a[mine]) - log_a[mine]
            p_c = jnp.exp(x_c)
            g_c = weight[mine] * p_c * (x_c - x_a - kl[mine])
            g_a = weight[mine] * (jnp.exp(x_a) - p_c)
            both = jnp.concatenate([g_c, g_a], axis=0)
            high = both.astype(BF16)
            slot = n % 2
            gbuf[slot, :tokens] = high
            gbuf[slot, tokens:] = (both - high.astype(F32)).astype(BF16)
            for side, start in ((1, far), (0, near)):
                for d in range(0, half, step):
                    out = lax.dot_general(
                        gbuf[slot],
                        wbuf[minus[i], pl.ds(pl.multiple_of(start + d, 128), step), :],
                        (((1,), (1,)), ((), ())),
                        preferred_element_type=F32,
                    )
                    out = out[:tokens] + out[tokens:]
                    if n == 0:
                        acc[g, side, :, d : d + step] = out
                    else:
                        acc[g, side, :, d : d + step] += out
                if side and n == n_xy - 1:
                    c1[g] = remote(acc.at[g, 1], core_in.at[g], c1_s.at[g], c1_r.at[g], partner)

    places = [
        (k * (n_hi // 2) + g * (n_hi // 4) + b, g, k * few + b * block)
        for g in range(2) for k in range(2) for b in range(n_hi // 4)
    ]

    def z_copy(to, g, row):
        return pltpu.make_async_remote_copy(
            src_ref=acc.at[g, 0, pl.ds(row, block)],
            dst_ref=z_in.at[hi],
            send_sem=z_s.at[to],
            recv_sem=z_r.at[hi],
            device_id=(px, py, to * 2 + lo),
            device_id_type=MESH,
        )

    def z_send(g):
        c1[g].wait_recv()
        acc[g, 0] += core_in[g]
        for to, which, row in places:
            if which == g:
                @pl.when(hi != to)
                def _():
                    z_copy(to, g, row).start()

                @pl.when(hi == to)
                def _():
                    z_in[to] = acc[g, 0, pl.ds(row, block), :]

    c1 = {}
    product(0)
    gather_forward(1)
    z_send(0)
    product(1)
    z_send(1)
    for source in range(n_hi):
        @pl.when(hi != source)
        def _():
            pltpu.make_async_remote_copy(
                src_ref=z_in.at[source], dst_ref=z_in.at[source],
                send_sem=z_s.at[source], recv_sem=z_r.at[source],
                device_id=(px, py, source * 2 + lo), device_id_type=MESH,
            ).wait_recv()
    z_own[...] = sum(z_in[j] for j in range(n_hi))
    c2 = remote(z_own, c2_in, c2_s, c2_r, partner)
    c2.wait_recv()
    out = block // 2
    first = lo == 0
    mine = jnp.where(first, z_own[:out], z_own[out:])
    theirs = jnp.where(first, c2_in[:out], c2_in[out:])
    grad_ref[:, :half] = jnp.where(first, mine, theirs)
    grad_ref[:, half:] = jnp.where(first, theirs, mine)

    for copy in [*rs.values(), *ag.values(), *sa.values(), *sb.values(), *c1.values(), c2]:
        copy.wait_send()
    for to, g, row in places:
        @pl.when(hi != to)
        def _():
            z_copy(to, g, row).wait_send()


def solution(mesh):
    n_pair, n_dp, n_v = (mesh.shape[a] for a in ("pair", "dp", "vocab"))
    n_xy, n_hi = n_pair * n_dp, n_v // 2

    def per_device(hidden, head_weight, answer_mask):
        tokens = hidden.shape[1]
        rows, few = 2 * tokens, tokens // 2
        depth, slab = head_weight.shape
        cols = slab // n_xy
        half = depth // 2
        block = rows // n_hi
        wide = -(-tokens // 128) * 128
        dma = pltpu.SemaphoreType.DMA
        vmem = pl.BlockSpec(memory_space=pltpu.VMEM)
        anywhere = pl.BlockSpec(memory_space=pl.ANY)
        grad, kl = pl.pallas_call(
            functools.partial(kernel, n_pair, n_dp, n_v),
            out_shape=(
                jax.ShapeDtypeStruct((rows // n_v, depth), F32),
                jax.ShapeDtypeStruct((1, tokens // n_dp), F32),
            ),
            in_specs=[anywhere] * 3,
            out_specs=(vmem, vmem),
            scratch_shapes=[
                pltpu.VMEM((rows, depth), BF16),
                pltpu.VMEM((1, tokens), jnp.int32),
                pltpu.VMEM((n_xy, depth, cols), BF16),
                pltpu.VMEM((2, n_xy, 2, few, cols), F32),
                pltpu.VMEM((2, n_xy, 2, few, cols), F32),
                pltpu.VMEM((2, n_xy, 2, few, cols), F32),
                pltpu.VMEM((2, rows, cols), BF16),
                pltpu.VMEM((n_v, 8, wide), F32),
                pltpu.VMEM((n_xy, 8, wide), F32),
                pltpu.VMEM((2, 2, tokens, half), F32),
                pltpu.VMEM((2, tokens, half), F32),
                pltpu.VMEM((n_hi, block, half), F32),
                pltpu.VMEM((block, half), F32),
                pltpu.VMEM((block, half), F32),
                dma((n_xy,)), dma((2,)),
                dma((2, n_xy)), dma((2, n_xy)),
                dma((2, n_xy, 2)), dma((2, n_xy, 2)),
                dma((n_v,)), dma((n_v,)),
                dma((n_xy,)), dma((n_xy,)),
                dma((2,)), dma((2,)),
                dma((n_hi,)), dma((n_hi,)),
                dma, dma,
            ],
            compiler_params=pltpu.CompilerParams(
                collective_id=0, has_side_effects=True, vmem_limit_bytes=48 * 2**20
            ),
        )(hidden.reshape(rows, depth), head_weight, answer_mask.reshape(1, tokens))
        return grad, kl.reshape(-1)

    return jax.shard_map(
        per_device,
        mesh=mesh,
        in_specs=(P(None, None, ("pair", "dp")), P(("pair", "dp"), "vocab"), P()),
        out_specs=(P("vocab", ("pair", "dp")), P("dp")),
        check_vma=False,
    )
```

```python
import functools

import jax
import jax.numpy as jnp
from jax import lax
from jax.experimental import pallas as pl
from jax.experimental.pallas import tpu as pltpu
from jax.sharding import PartitionSpec as P

trades_scale = 6.0
MESH = pl.DeviceIdType.MESH
F32 = jnp.float32
BF16 = jnp.bfloat16


def merge(parts):
    top_c = functools.reduce(jnp.maximum, [p[0] for p in parts])
    top_a = functools.reduce(jnp.maximum, [p[3] for p in parts])
    total_c = total_a = cross = 0.0
    for m_c, s_c, t, m_a, s_a in parts:
        down_c, down_a = m_c - top_c, m_a - top_a
        e_c = jnp.exp(down_c)
        total_c += e_c * s_c
        total_a += jnp.exp(down_a) * s_a
        cross += e_c * (t + s_c * (down_c - down_a))
    return top_c, total_c, cross, top_a, total_a


def pack(stats):
    place = lax.broadcasted_iota(jnp.int32, (8, stats[0].shape[1]), 0)
    out = jnp.zeros(place.shape, F32)
    for j, s in enumerate(stats):
        out = jnp.where(place == j, s, out)
    return out


def unpack(value):
    return tuple(value[j : j + 1, :] for j in range(5))


def kernel(
    n_pair, n_dp, n_v,
    h_any, w_ref, mask_any,
    grad_ref, kl_ref,
    h_ref, mask_ref, wbuf, part, rs_in, gath, gbuf, st_a, st_b, acc, core_in, z_in, z_own, c2_in,
    w_sem, in_sem, rs_s, rs_r, ag_s, ag_r, sa_s, sa_r, sb_s, sb_r, c1_s, c1_r, z_s, z_r, c2_s, c2_r,
):
    n_xy = n_pair * n_dp
    n_hi = n_v // 2
    rows, depth = h_ref.shape
    tokens = rows // 2
    few = tokens // 2
    wide = st_a.shape[2]
    cols = wbuf.shape[2]
    half = depth // 2
    block = rows // n_hi
    px, py, v = lax.axis_index("pair"), lax.axis_index("dp"), lax.axis_index("vocab")
    hi, lo = v // 2, v % 2

    shifts = [(i // n_dp, i % n_dp) for i in range(n_xy)]
    peers = [
        (lax.rem(px + sx, n_pair), lax.rem(py + sy, n_dp)) for sx, sy in shifts
    ]
    minus = [((-sx) % n_pair) * n_dp + (-sy) % n_dp for sx, sy in shifts]
    along_x = [sx * n_dp for sx in range(1, n_pair)]
    along_y = list(range(1, n_dp))
    across = [i for i in range(n_xy) if shifts[i][0] and shifts[i][1]]
    order = across + along_x + along_y + [0]

    def xy_id(i):
        return (peers[i][0], peers[i][1], v)

    def v_id(j):
        return (px, py, lax.rem(v + j, n_v))

    partner = (px, py, hi * 2 + (1 - lo))

    h_load = pltpu.make_async_copy(h_any, h_ref, in_sem.at[0])
    h_load.start()
    loads = {}
    for i in order:
        q = peers[i][0] * n_dp + peers[i][1]
        loads[i] = pltpu.make_async_copy(
            w_ref.at[:, pl.ds(pl.multiple_of(q * cols, 128), cols)], wbuf.at[i], w_sem.at[i]
        )
        loads[i].start()
    mask_load = pltpu.make_async_copy(mask_any, mask_ref, in_sem.at[1])
    mask_load.start()

    barrier = pltpu.get_barrier_semaphore()
    for i in range(1, n_xy):
        pl.semaphore_signal(barrier, inc=1, device_id=xy_id(i), device_id_type=MESH)
    for j in range(1, n_v):
        pl.semaphore_signal(barrier, inc=1, device_id=v_id(j), device_id_type=MESH)

    def remote(src, dst, send, recv, to):
        copy = pltpu.make_async_remote_copy(
            src_ref=src, dst_ref=dst, send_sem=send, recv_sem=recv, device_id=to, device_id_type=MESH
        )
        copy.start()
        return copy

    rs = {}

    def reduce_send(g, i, to):
        rs[g, i] = remote(part.at[g, i], rs_in.at[g, i], rs_s.at[g, i], rs_r.at[g, i], xy_id(to))

    h_load.wait()
    for n, i in enumerate(order):
        sx, sy = shifts[i]
        loads[i].wait()
        value = jnp.dot(h_ref[...], wbuf[i], preferred_element_type=F32)
        for g in range(2):
            for k in range(2):
                part[g, i, k] = value[k * tokens + g * few : k * tokens + (g + 1) * few]
        if n == 0:
            pl.semaphore_wait(barrier, n_xy - 1 + n_v - 1)
        if sx:
            reduce_send(0, i, sx * n_dp)
        if sy:
            reduce_send(1, i, sy)

    def take(g, i, source):
        rs[g, source].wait_recv()
        part[g, i] += rs_in[g, source]

    for sy in along_y:
        for sx in range(1, n_pair):
            take(0, sy, sx * n_dp + sy)
        reduce_send(0, sy, sy)
    for i in along_x:
        for sy in along_y:
            take(1, i, i + sy)
        reduce_send(1, i, i)

    ag = {}

    def gather_send(g):
        for i in along_x + along_y:
            ag[g, i, 0] = remote(
                gath.at[g, 0], gath.at[g, i], ag_s.at[g, i, 0], ag_r.at[g, i, 0], xy_id(i)
            )

    def gather_forward(g):
        for sy in along_y:
            ag[g, sy, 0].wait_recv()
            for i in along_x:
                ag[g, i + sy, 0] = remote(
                    gath.at[g, sy, 0], gath.at[g, i + sy, 0],
                    ag_s.at[g, i + sy, 0], ag_r.at[g, i + sy, 0], xy_id(i),
                )
        for i in along_x:
            ag[g, i, 0].wait_recv()
            for sy in along_y:
                ag[g, i + sy, 1] = remote(
                    gath.at[g, i, 1], gath.at[g, i + sy, 1],
                    ag_s.at[g, i + sy, 1], ag_r.at[g, i + sy, 1], xy_id(sy),
                )

    for i in along_x:
        take(0, 0, i)
    for i in along_y:
        take(1, 0, i)
    for i in along_y:
        rs[0, i].wait_recv()
    gath[0, 0] = part[0, 0] + sum(rs_in[0, i] for i in along_y)
    gather_send(0)
    for i in along_x:
        rs[1, i].wait_recv()
    gath[1, 0] = part[1, 0] + sum(rs_in[1, i] for i in along_x)

    diagonal = lax.broadcasted_iota(jnp.int32, (tokens, wide), 0) == lax.broadcasted_iota(
        jnp.int32, (tokens, wide), 1
    )

    def to_row(column):
        return jnp.sum(jnp.where(diagonal, column, 0.0), axis=0, keepdims=True)

    def to_column(row):
        return jnp.sum(jnp.where(diagonal, row, 0.0), axis=1, keepdims=True)

    l_c = jnp.concatenate([gath[0, 0, 0], gath[1, 0, 0]], axis=0)
    l_a = jnp.concatenate([gath[0, 0, 1], gath[1, 0, 1]], axis=0)
    m_c = jnp.max(l_c, axis=1, keepdims=True)
    m_a = jnp.max(l_a, axis=1, keepdims=True)
    l_c, l_a = l_c - m_c, l_a - m_a
    e_c = jnp.exp(l_c)
    stats = (
        m_c,
        jnp.sum(e_c, axis=1, keepdims=True),
        jnp.sum(e_c * (l_c - l_a), axis=1, keepdims=True),
        m_a,
        jnp.sum(jnp.exp(l_a), axis=1, keepdims=True),
    )
    st_a[0] = pack([to_row(s) for s in stats])
    sa = {}
    for j in range(1, n_v):
        sa[j] = remote(st_a.at[0], st_a.at[j], sa_s.at[j], sa_r.at[j], v_id(j))
    for j in range(1, n_v):
        sa[j].wait_recv()
    st_b[0] = pack(merge([unpack(st_a[j]) for j in range(n_v)]))
    sb = {}
    for i in range(1, n_xy):
        sb[i] = remote(st_b.at[0], st_b.at[i], sb_s.at[i], sb_r.at[i], xy_id(i))
    gather_forward(0)
    gather_send(1)

    mask_load.wait()
    mask = jnp.sum(
        jnp.where(diagonal[:, :tokens], mask_ref[...].astype(F32), 0.0), axis=1, keepdims=True
    )
    weight = trades_scale * mask
    for i in range(1, n_xy):
        sb[i].wait_recv()
    joined = merge([unpack(st_b[i]) for i in range(n_xy)])
    top_c, total_c, cross, top_a, total_a = (to_column(s) for s in joined)
    log_c, log_a = jnp.log(total_c), jnp.log(total_a)
    kl = cross / total_c - log_c + log_a
    group = kl_ref.shape[1]
    token = lax.broadcasted_iota(jnp.int32, (tokens, group), 0)
    place = lax.broadcasted_iota(jnp.int32, (tokens, group), 1) + py * group
    kl_ref[...] = jnp.sum(jnp.where(token == place, mask * kl, 0.0), axis=0, keepdims=True)

    step = min(512, half)
    near = pl.multiple_of(lo * half, 128)
    far = pl.multiple_of((1 - lo) * half, 128)

    def product(g):
        mine = slice(g * few, (g + 1) * few)
        for n, i in enumerate([0] + along_y + along_x + across):
            if i in across:
                ag[g, i, 0].wait_recv()
                ag[g, i, 1].wait_recv()
            x_c = (gath[g, i, 0] - top_c[mine]) - log_c[mine]
            x_a = (gath[g, i, 1] - top_a[mine]) - log_a[mine]
            p_c = jnp.exp(x_c)
            g_c = weight[mine] * p_c * (x_c - x_a - kl[mine])
            g_a = weight[mine] * (jnp.exp(x_a) - p_c)
            both = jnp.concatenate([g_c, g_a], axis=0)
            high = both.astype(BF16)
            slot = n % 2
            gbuf[slot, :tokens] = high
            gbuf[slot, tokens:] = (both - high.astype(F32)).astype(BF16)
            for side, start in ((1, far), (0, near)):
                for d in range(0, half, step):
                    out = lax.dot_general(
                        gbuf[slot],
                        wbuf[minus[i], pl.ds(pl.multiple_of(start + d, 128), step), :],
                        (((1,), (1,)), ((), ())),
                        preferred_element_type=F32,
                    )
                    out = out[:tokens] + out[tokens:]
                    if n == 0:
                        acc[g, side, :, d : d + step] = out
                    else:
                        acc[g, side, :, d : d + step] += out
                    if side and n == n_xy - 1:
                        c1[g, d] = remote(
                            acc.at[g, 1, :, pl.ds(d, step)], core_in.at[g, :, pl.ds(d, step)],
                            c1_s.at[g, d // step], c1_r.at[g, d // step], partner,
                        )

    places = [
        (k * (n_hi // 2) + g * (n_hi // 4) + b, g, k * few + b * block)
        for g in range(2) for k in range(2) for b in range(n_hi // 4)
    ]
    places.sort(key=lambda place: min(place[0], n_hi - 1 - place[0]))

    def z_copy(to, g, row, d):
        return pltpu.make_async_remote_copy(
            src_ref=acc.at[g, 0, pl.ds(row, block), pl.ds(d, step)],
            dst_ref=z_in.at[hi, :, pl.ds(d, step)],
            send_sem=z_s.at[to, d // step],
            recv_sem=z_r.at[hi, d // step],
            device_id=(px, py, to * 2 + lo),
            device_id_type=MESH,
        )

    def z_send(g):
        for d in range(0, half, step):
            c1[g, d].wait_recv()
            acc[g, 0, :, d : d + step] += core_in[g, :, d : d + step]
            for to, which, row in places:
                if which == g:
                    @pl.when(hi != to)
                    def _():
                        z_copy(to, g, row, d).start()

                    @pl.when(hi == to)
                    def _():
                        z_in[to, :, d : d + step] = acc[g, 0, pl.ds(row, block), d : d + step]

    c1 = {}
    product(0)
    gather_forward(1)
    z_send(0)
    product(1)
    z_send(1)
    for source, d in [(j, d) for j in range(n_hi) for d in range(0, half, step)]:
        @pl.when(hi != source)
        def _():
            pltpu.make_async_remote_copy(
                src_ref=z_in.at[source, :, pl.ds(d, step)], dst_ref=z_in.at[source, :, pl.ds(d, step)],
                send_sem=z_s.at[source, d // step], recv_sem=z_r.at[source, d // step],
                device_id=(px, py, source * 2 + lo), device_id_type=MESH,
            ).wait_recv()
    z_own[...] = sum(z_in[j] for j in range(n_hi))
    c2 = remote(z_own, c2_in, c2_s, c2_r, partner)
    c2.wait_recv()
    out = block // 2
    first = lo == 0
    mine = jnp.where(first, z_own[:out], z_own[out:])
    theirs = jnp.where(first, c2_in[:out], c2_in[out:])
    grad_ref[:, :half] = jnp.where(first, mine, theirs)
    grad_ref[:, half:] = jnp.where(first, theirs, mine)

    for copy in [*rs.values(), *ag.values(), *sa.values(), *sb.values(), *c1.values(), c2]:
        copy.wait_send()
    for to, g, row in places:
        @pl.when(hi != to)
        def _():
            for d in range(0, half, step):
                z_copy(to, g, row, d).wait_send()


def solution(mesh):
    n_pair, n_dp, n_v = (mesh.shape[a] for a in ("pair", "dp", "vocab"))
    n_xy, n_hi = n_pair * n_dp, n_v // 2

    def per_device(hidden, head_weight, answer_mask):
        tokens = hidden.shape[1]
        rows, few = 2 * tokens, tokens // 2
        depth, slab = head_weight.shape
        cols = slab // n_xy
        half = depth // 2
        block = rows // n_hi
        pieces = half // min(512, half)
        wide = -(-tokens // 128) * 128
        dma = pltpu.SemaphoreType.DMA
        vmem = pl.BlockSpec(memory_space=pltpu.VMEM)
        anywhere = pl.BlockSpec(memory_space=pl.ANY)
        grad, kl = pl.pallas_call(
            functools.partial(kernel, n_pair, n_dp, n_v),
            out_shape=(
                jax.ShapeDtypeStruct((rows // n_v, depth), F32),
                jax.ShapeDtypeStruct((1, tokens // n_dp), F32),
            ),
            in_specs=[anywhere] * 3,
            out_specs=(vmem, vmem),
            scratch_shapes=[
                pltpu.VMEM((rows, depth), BF16),
                pltpu.VMEM((1, tokens), jnp.int32),
                pltpu.VMEM((n_xy, depth, cols), BF16),
                pltpu.VMEM((2, n_xy, 2, few, cols), F32),
                pltpu.VMEM((2, n_xy, 2, few, cols), F32),
                pltpu.VMEM((2, n_xy, 2, few, cols), F32),
                pltpu.VMEM((2, rows, cols), BF16),
                pltpu.VMEM((n_v, 8, wide), F32),
                pltpu.VMEM((n_xy, 8, wide), F32),
                pltpu.VMEM((2, 2, tokens, half), F32),
                pltpu.VMEM((2, tokens, half), F32),
                pltpu.VMEM((n_hi, block, half), F32),
                pltpu.VMEM((block, half), F32),
                pltpu.VMEM((block, half), F32),
                dma((n_xy,)), dma((2,)),
                dma((2, n_xy)), dma((2, n_xy)),
                dma((2, n_xy, 2)), dma((2, n_xy, 2)),
                dma((n_v,)), dma((n_v,)),
                dma((n_xy,)), dma((n_xy,)),
                dma((2, pieces)), dma((2, pieces)),
                dma((n_hi, pieces)), dma((n_hi, pieces)),
                dma, dma,
            ],
            compiler_params=pltpu.CompilerParams(
                collective_id=0, has_side_effects=True, vmem_limit_bytes=48 * 2**20
            ),
        )(hidden.reshape(rows, depth), head_weight, answer_mask.reshape(1, tokens))
        return grad, kl.reshape(-1)

    return jax.shard_map(
        per_device,
        mesh=mesh,
        in_specs=(P(None, None, ("pair", "dp")), P(("pair", "dp"), "vocab"), P()),
        out_specs=(P("vocab", ("pair", "dp")), P("dp")),
        check_vma=False,
    )
```
